256 devices in a mesh: outer: 4 (over y_hi, core), inner: 16 (over y_lo, z), head: 4 (over x).
Axes of the slice: x: 4, y: 4 (y_hi: 2, y_lo: 2; y = y_hi * 2 + y_lo), z: 8, core: 2. Of those that a mesh axis runs over, the one named last changes fastest.
Arguments:
- queries: bfloat16 [32768, 24, 128], P(('outer', 'inner', 'head')), may hold values from -6 to 6
- keys: bfloat16 [32768, 4, 128], P(('outer', 'inner', 'head')), may hold values from -6 to 6
- values: bfloat16 [32768, 4, 128], P(('outer', 'inner', 'head')), may hold values from -6 to 6
- block_order: int32 [128], replicated, may hold values from 0 to 127, each once
Outputs:
- attended: bfloat16 [32768, 24, 128], P(('outer', 'inner', 'head'))
- log_sum: float32 [24, 32768], P('head', ('outer', 'inner'))
The draws below stay inside these ranges and needn't reach their ends.
Inputs may be any that keep to these rules, and one draw needn't show every extreme that they name: block_order names each half block once.
All inputs are finite; a program needn't handle non-finite values.
Results may differ from the reference program's by a relative error of at most 0.007.
Values may be sent and summed in bfloat16 or wider, within the bound.
A program may use at most 64 MiB of HBM per device.

```python
import math
import jax
import jax.numpy as jnp
from jax import lax

HQ = 24
HK = 4
HD = 128
ROWS = 512
HALF = 256
NBLK = 128
TOKENS = 32768
N_OUTER = 4
N_INNER = 16


def base_draw(key, shape):
    return jnp.clip(jax.random.normal(key, shape, jnp.float32), -6.0, 6.0)


def draw_queries(key, part):
    key = jax.random.fold_in(key, 11)
    drawn = base_draw(key, (TOKENS, HQ, HD))
    return drawn.astype(jnp.bfloat16)


def draw_keys(key, part):
    key = jax.random.fold_in(key, 13)
    drawn = base_draw(key, (TOKENS, HK, HD))
    return drawn.astype(jnp.bfloat16)


def level_of(key, extent, pieces, least, top_value):
    level = 1.0
    for position, parts in pieces:
        draws = jax.random.uniform(jax.random.fold_in(jax.random.fold_in(key, 6), position), (parts,), jnp.float32, least / len(pieces), top_value / len(pieces))
        level = level * jnp.repeat(jnp.exp(draws), extent[position] // parts).reshape((-1,) + (1,) * (len(extent) - 1 - position))
    return level


def normal_values(own_key, extent, deviation, reach, cuts=(), kind=jnp.bfloat16):
    loudness = level_of(own_key, extent, cuts, -0.22, 0.18) if cuts else 1.0
    values = jax.random.normal(own_key, extent, jnp.float32) * deviation * loudness
    return jnp.minimum(jnp.maximum(values, -reach), reach).astype(kind)


def setup_inputs(seed: int = 0) -> dict:
    key_list = jax.random.split(jax.random.key(seed), 5)
    queries = draw_queries(jax.random.fold_in(key_list[4], 71), 0)
    keys = draw_keys(jax.random.fold_in(key_list[4], 71), 0)
    values = normal_values(key_list[2], (TOKENS, HK, HD), 1.0, 6.0, ((0, 256),))
    block_order = jax.random.permutation(key_list[3], NBLK).astype(jnp.int32)
    return dict(queries=queries, keys=keys, values=values, block_order=block_order)


def storage_positions(block_order, first_row, row_total):
    row_ids = first_row + jnp.arange(row_total, dtype=jnp.int32)
    owners = row_ids // HALF
    table = jnp.arange(block_order.shape[0], dtype=jnp.int32)
    picked = lax.optimization_barrier(jnp.sum(jnp.where(owners[:, None] == table[None, :], block_order[None, :], 0), axis=1))
    return (picked * HALF + row_ids % HALF).astype(jnp.int32)

def reference(queries, keys, values, block_order):
    group = HQ // HK
    score_scale = 1.0 / math.sqrt(HD)
    blocks = N_OUTER * N_INNER
    pos_all = storage_positions(block_order, jnp.int32(0), TOKENS)
    q_blocks = queries.reshape(blocks, ROWS, HK, group, HD)
    k_own = keys.reshape(blocks, ROWS, HK, HD)
    v_own = values.reshape(blocks, ROWS, HK, HD)
    k_seg = keys.reshape(N_OUTER, N_INNER * ROWS, HK, HD)
    v_seg = values.reshape(N_OUTER, N_INNER * ROWS, HK, HD)
    p_blocks = pos_all.reshape(blocks, ROWS)
    p_seg = pos_all.reshape(N_OUTER, N_INNER * ROWS)

    def one_block(block_id):
        previous = (block_id // N_INNER + N_OUTER - 1) % N_OUTER
        q_float = q_blocks[block_id].astype(jnp.float32)
        k_float = jnp.concatenate([k_own[block_id], k_seg[previous]], 0).astype(jnp.float32)
        v_float = jnp.concatenate([v_own[block_id], v_seg[previous]], 0).astype(jnp.float32)
        k_pos = jnp.concatenate([p_blocks[block_id], p_seg[previous]], 0)
        q_pos = p_blocks[block_id]
        scores = jnp.einsum('qhgd,khd->hgqk', q_float, k_float) * score_scale
        visible = k_pos[None, :] <= q_pos[:, None]
        scores = jnp.where(visible, scores, -jnp.inf)
        row_max = lax.optimization_barrier(jnp.max(scores, axis=-1))
        powers = jnp.exp(scores - row_max[..., None])
        totals = lax.optimization_barrier(jnp.sum(powers, axis=-1))
        rounded = lax.optimization_barrier(powers.astype(jnp.bfloat16))
        weighted = jnp.einsum('hgqk,khd->hgqd', rounded.astype(jnp.float32), v_float)
        normalized = weighted / totals[..., None]
        out_rows = jnp.transpose(normalized, (2, 0, 1, 3)).reshape(ROWS, HQ, HD).astype(jnp.bfloat16)
        log_rows = (row_max + jnp.log(totals)).reshape(HQ, ROWS)
        return (out_rows, log_rows)
    outs, logs = lax.map(one_block, jnp.arange(blocks, dtype=jnp.int32))
    attended = outs.reshape(TOKENS, HQ, HD)
    log_sum = jnp.transpose(logs, (1, 0, 2)).reshape(HQ, TOKENS)
    return (attended, log_sum)
```

```python
import functools
import math

import jax
import jax.numpy as jnp
from jax import lax
from jax.experimental import pallas as pl
from jax.experimental.pallas import tpu as pltpu
from jax.sharding import PartitionSpec as P

MESH = pl.DeviceIdType.MESH
NEG = -1e30
LN2 = math.log(2.0)
NT = (((1,), (1,)), ((), ()))
NN = (((1,), (0,)), ((), ()))
ARRIVAL = (0, 1, 3, 2)
ORDER = (2, 1, 3, 0)


def kernel(
    group, ring, order_ref, q_in, kv_in, out_ref, log_ref,
    qbuf, own, kbuf, vbuf, outbuf, m_ref, acc_ref, s0, s1, tile_max,
    q_send, q_recv, x_send, x_recv, first_send, k_recv, v_recv, k_send, v_send, y_send,
    o_send, o_recv,
):
    outer, inner, head = (lax.axis_index(a) for a in ("outer", "inner", "head"))
    outers, heads = lax.axis_size("outer"), lax.axis_size("head")
    inners = lax.axis_size("inner")
    y, z = inner // ring, inner % ring
    part = q_in.shape[1] // group
    half = 2 * part
    keys = heads * part
    head_dim = q_in.shape[2]
    scale = math.log2(math.e) / math.sqrt(head_dim)
    core = outer % 2
    turn = 2 * core - 1
    after, before = (outer + 1) % outers, (outer + outers - 1) % outers
    near = jnp.where(core == 0, y, 1 - y)

    def at_head(by):
        return (outer, inner, (head + by) % heads)

    def at_next(y_there):
        return (after, y_there * ring + z, head)

    def at_z(by):
        return (outer, y * ring + (z + by + ring) % ring, head)

    y_peer = (outer, (1 - y) * ring + z, head)

    barrier = pltpu.get_barrier_semaphore()
    peers = [at_head(r) for r in (1, 2, 3)]
    peers += [at_next(0), at_next(1), (before, z, head), (before, ring + z, head)]
    peers += [at_z(1), at_z(-1), y_peer]
    for peer in peers:
        pl.semaphore_signal(barrier, inc=1, device_id=peer, device_id_type=MESH)
    pl.semaphore_wait(barrier, len(peers))

    def remote(src, dst, send, recv, peer):
        return pltpu.make_async_remote_copy(
            src_ref=src, dst_ref=dst, send_sem=send, recv_sem=recv,
            device_id=peer, device_id_type=MESH,
        )

    def kv_copy(r):
        there = (head + r) % heads
        return remote(kv_in.at[there], own.at[:, head], x_send.at[r], x_recv.at[r], at_head(r))

    def q_copy(r):
        there = (head + r) % heads
        return remote(q_in.at[there], qbuf.at[heads - r], q_send.at[r], q_recv.at[r], at_head(r))

    for r in (2, 1, 3):
        kv_copy(r).start()
    for r in (1, 3, 2):
        q_copy(r).start()
    own[0, head] = kv_in[head, 0]
    own[1, head] = kv_in[head, 1]
    qbuf[0] = q_in[head]
    m_ref[...] = jnp.full(m_ref.shape, NEG, jnp.float32)
    acc_ref[...] = jnp.zeros(acc_ref.shape, jnp.float32)
    for r in (1, 2, 3):
        kv_copy(r).wait_recv()

    def first_copies():
        return (
            remote(own.at[1], vbuf.at[0, z], first_send.at[0], v_recv.at[0, z], at_next(near)),
            remote(own.at[0], kbuf.at[0, z], first_send.at[1], k_recv.at[0, z], at_next(near)),
            remote(own.at[0], kbuf.at[1, z], first_send.at[2], k_recv.at[1, z], at_next(1 - near)),
        )

    for copy in first_copies():
        copy.start()

    def k_copy(way, kind, origin):
        peer = at_z(turn if way == 0 else -turn)
        return remote(
            kbuf.at[kind, origin], kbuf.at[kind, origin],
            k_send.at[way, kind, origin], k_recv.at[kind, origin], peer,
        )

    def v_copy(way, origin):
        peer = at_z(turn if way == 0 else -turn)
        return remote(
            vbuf.at[0, origin], vbuf.at[0, origin],
            v_send.at[way, origin], v_recv.at[0, origin], peer,
        )

    def y_copy(origin):
        return remote(
            vbuf.at[0, origin], vbuf.at[1, origin], y_send.at[origin], v_recv.at[1, origin], y_peer
        )

    def origin_of(way, step):
        by = turn * step
        return (z - by + ring) % ring if way == 0 else (z + by + ring) % ring

    def arrive_first():
        v_copy(0, z).wait_recv()
        v_copy(0, z).start()
        v_copy(1, z).start()
        y_copy(z).start()
        k_copy(0, 0, z).wait_recv()
        k_copy(0, 0, z).start()
        k_copy(1, 0, z).start()
        k_copy(0, 1, z).wait_recv()
        k_copy(0, 1, z).start()
        k_copy(1, 1, z).start()

    def last_step(way, kind):
        return ring // 2 if way == kind else ring // 2 - 1

    def arrive_from(way, kind, step, do):
        origin = origin_of(way, step)
        go = do == "go"
        onward = step < last_step(way, kind)
        if go:
            if kind == 0:
                v_copy(way, origin).wait_recv()
            k_copy(way, kind, origin).wait_recv()
        if kind == 0:
            if go:
                y_copy(origin).start()
            else:
                y_copy(origin).wait_send()

        def pass_on():
            if go:
                if kind == 0:
                    v_copy(way, origin).start()
                k_copy(way, kind, origin).start()
            else:
                if kind == 0:
                    v_copy(way, origin).wait_send()
                k_copy(way, kind, origin).wait_send()

        pl.when(onward)(pass_on)
        if go and kind == 1:
            remote(
                vbuf.at[1, origin], vbuf.at[1, origin], y_send.at[origin],
                v_recv.at[1, origin], y_peer,
            ).wait_recv()

    def arrive(c, do="go"):
        step, place = c // 4, c % 4
        for way in (0, 1):
            for kind in (0, 1):
                pl.when(place == 2 * kind + way)(
                    functools.partial(arrive_from, way, kind, step, do)
                )

    def slot_of(c):
        step, place = c // 4, c % 4
        kind = jnp.where(step == 0, place - 2, jnp.where(step == ring // 2, place, place // 2))
        sign = 1 - 2 * (place % 2)
        return kind, (z - turn * sign * step + ring) % ring

    def halves_of(c):
        kind, origin = slot_of(c)
        y_there = jnp.where((core + kind) % 2 == 1, y, 1 - y)
        block = before * inners + y_there * ring + origin
        return order_ref[2 * block], order_ref[2 * block + 1]

    here = 2 * (outer * inners + inner)
    here_order = (order_ref[here], order_ref[here + 1])

    def tile_order(r):
        return jnp.where((head + r) % heads < 2, here_order[0], here_order[1])

    scores = (s0, s1)
    columns = group * part

    def score(k_rows, r):
        q = qbuf[r]
        return lax.dot_general(k_rows, q, NT, preferred_element_type=jnp.float32) * scale

    def ahead(c, r, slot):
        kind, origin = slot_of(c)
        for h in range(2):
            k_rows = kbuf[kind, origin, 2 * h : 2 * h + 2].reshape(half, head_dim)
            s = score(k_rows, r)
            scores[slot][h * half : (h + 1) * half] = s
            tile_max[slot, h] = jnp.max(s, axis=0, keepdims=True)

    def ahead_own(r, slot):
        token = lax.broadcasted_iota(jnp.int32, (1, columns), 1) % part
        q_token = ((head + r) % 2) * part + token
        q_pos = tile_order(r) * half + q_token
        for h in range(2):
            k_rows = own[0, 2 * h : 2 * h + 2].reshape(half, head_dim)
            k_pos = here_order[h] * half + lax.broadcasted_iota(jnp.int32, (half, 1), 0)
            s = jnp.where(k_pos <= q_pos, score(k_rows, r), NEG)
            scores[slot][h * half : (h + 1) * half] = s
            tile_max[slot, h] = jnp.max(s, axis=0, keepdims=True)

    def absorb(v_parts, hidden, r, slot):
        old = m_ref[r]
        new = old
        for h in range(2):
            new = jnp.maximum(new, tile_max[slot, h] - hidden[h])
        shrink = jnp.exp2(old - new)
        m_ref[r] = new
        weights = jnp.concatenate(
            [
                jnp.exp2(scores[slot][h * half : (h + 1) * half] - (new + hidden[h]))
                for h in range(2)
            ],
            axis=0,
        ).astype(jnp.bfloat16)
        v = jnp.concatenate(v_parts, axis=1)
        v = jnp.concatenate([v, jnp.ones((16, keys), jnp.bfloat16)], axis=0)
        add = lax.dot_general(v, weights, NN, preferred_element_type=jnp.float32)
        acc_ref[r] = acc_ref[r] * shrink + add[: head_dim + 8]

    def now(c, r, slot):
        kind, origin = slot_of(c)
        mine = tile_order(r)
        hidden = [jnp.where(k < mine, 0.0, -NEG) for k in halves_of(c)]
        absorb([vbuf[kind, origin, x] for x in range(heads)], hidden, r, slot)

    def now_own(r, slot):
        absorb([own[1, x] for x in range(heads)], (0.0, 0.0), r, slot)

    def out_copy(r):
        return remote(
            outbuf.at[r], out_ref.at[head], o_send.at[r], o_recv.at[r], at_head(r)
        )

    def finish(r):
        total = acc_ref[r, head_dim : head_dim + 1]
        rows = (acc_ref[r, :head_dim] / total).T.astype(jnp.bfloat16)
        there = (head + r) % heads
        if r == 0:
            out_ref[head] = rows
        else:
            outbuf[r] = rows
            out_copy(r).start()
        logs = (m_ref[r] + jnp.log2(total)) * LN2
        for g in range(group):
            log_ref[g : g + 1, pl.ds(pl.multiple_of(there * part, part), part)] = logs[
                :, g * part : (g + 1) * part
            ]

    ahead_own(ARRIVAL[0], 0)
    for n, r in enumerate(ARRIVAL):
        if n == 1:
            arrive_first()
        if n < 3:
            q_copy(heads - ARRIVAL[n + 1]).wait_recv()
            ahead_own(ARRIVAL[n + 1], (n + 1) % 2)
        else:
            ahead(2, ORDER[0], 0)
        now_own(r, n % 2)

    remote(
        vbuf.at[1, z], vbuf.at[1, z], y_send.at[z], v_recv.at[1, z], y_peer
    ).wait_recv()

    def chunk(c, _):
        for n, r in enumerate(ORDER):
            if n == 2:
                pl.when(jnp.logical_and(c >= 3, c < 15))(lambda: arrive(c + 1))
                pl.when(c == 15)(lambda: arrive_from(0, 0, ring // 2, "go"))
            if n < 3:
                ahead(c, ORDER[n + 1], (n + 1) % 2)
            else:
                ahead(c + 1, ORDER[0], 0)
            now(c, r, n % 2)
        return 0

    lax.fori_loop(2, 16, chunk, 0)
    arrive_from(1, 1, ring // 2, "go")
    for n, r in enumerate(ORDER):
        ahead(17, r, 1)
        now(16, r, 0)
        if n < 3:
            ahead(16, ORDER[n + 1], 0)
        now(17, r, 1)
        finish(r)

    for r in (1, 2, 3):
        out_copy(r).wait_recv()
    for r in (1, 2, 3):
        out_copy(r).wait_send()
        kv_copy(r).wait_send()
        q_copy(r).wait_send()
    for copy in first_copies():
        copy.wait_send()
    y_copy(z).wait_send()
    for way in (0, 1):
        v_copy(way, z).wait_send()
        for kind in (0, 1):
            k_copy(way, kind, z).wait_send()

    def ended(c, _):
        arrive(c, "end")
        return 0

    lax.fori_loop(4, 16, ended, 0)
    y_copy(origin_of(0, ring // 2)).wait_send()


def body(queries, keys, values, block_order):
    heads = lax.axis_size("head")
    inners = lax.axis_size("inner")
    part, q_heads, head_dim = queries.shape
    group = q_heads // heads
    ring = inners // 2
    columns = group * part
    q_in = jnp.transpose(queries, (1, 0, 2)).reshape(heads, columns, head_dim)
    kv_in = jnp.stack([jnp.transpose(keys, (1, 0, 2)), jnp.transpose(values, (1, 2, 0))], axis=1)
    block = heads * part
    bf16, f32 = jnp.bfloat16, jnp.float32
    dma = pltpu.SemaphoreType.DMA
    vmem = pl.BlockSpec(memory_space=pltpu.VMEM)
    rows, logs = pl.pallas_call(
        functools.partial(kernel, group, ring),
        out_shape=(
            jax.ShapeDtypeStruct((heads, columns, head_dim), bf16),
            jax.ShapeDtypeStruct((group, block), f32),
        ),
        in_specs=[pl.BlockSpec(memory_space=pltpu.SMEM), vmem, vmem],
        out_specs=(vmem, vmem),
        scratch_shapes=[
            pltpu.VMEM((heads, columns, head_dim), bf16),
            pltpu.VMEM((2, heads, part, head_dim), bf16),
            pltpu.VMEM((2, ring, heads, part, head_dim), bf16),
            pltpu.VMEM((2, ring, heads, head_dim, part), bf16),
            pltpu.VMEM((heads, columns, head_dim), bf16),
            pltpu.VMEM((heads, 1, columns), f32),
            pltpu.VMEM((heads, head_dim + 8, columns), f32),
            pltpu.VMEM((block, columns), f32),
            pltpu.VMEM((block, columns), f32),
            pltpu.VMEM((2, 2, 1, columns), f32),
            dma((heads,)),
            dma((heads,)),
            dma((heads,)),
            dma((heads,)),
            dma((3,)),
            dma((2, ring)),
            dma((2, ring)),
            dma((2, 2, ring)),
            dma((2, ring)),
            dma((ring,)),
            dma((heads,)),
            dma((heads,)),
        ],
        compiler_params=pltpu.CompilerParams(
            collective_id=0, has_side_effects=True, vmem_limit_bytes=48 * 2**20
        ),
        cost_estimate=pl.CostEstimate(
            flops=4 * q_heads * block * (2 * ring + 1) * block * head_dim // heads,
            bytes_accessed=4 * 2**20,
            transcendentals=q_heads * block * (2 * ring + 1) * block // heads,
        ),
    )(block_order, q_in, kv_in)
    attended = jnp.transpose(rows.reshape(q_heads, part, head_dim), (1, 0, 2))
    return attended, logs


def solution(mesh):
    spread = P(("outer", "inner", "head"), None, None)
    return jax.shard_map(
        body,
        mesh=mesh,
        in_specs=(spread, spread, spread, P()),
        out_specs=(spread, P("head", ("outer", "inner"))),
        check_vma=False,
    )
```

```python
import functools
import math

import jax
import jax.numpy as jnp
from jax import lax
from jax.experimental import pallas as pl
from jax.experimental.pallas import tpu as pltpu
from jax.sharding import PartitionSpec as P

MESH = pl.DeviceIdType.MESH
NEG = -1e30
LN2 = math.log(2.0)
NT = (((1,), (1,)), ((), ()))
NN = (((1,), (0,)), ((), ()))
ARRIVAL = (0, 1, 3, 2)
LOOP = (1, 3, 0, 2)
ORDER = (2, 1, 3, 0)
K1_PLACE = 1


def kernel(
    group, ring, order_ref, q_in, kv_in, out_ref, log_ref,
    qbuf, own, kbuf, vbuf, outbuf, m_ref, acc_ref, s0, s1, tile_max,
    q_send, q_recv, x_send, x_recv, first_send, first_recv, k_recv, v_recv, k_send, v_send, y_send,
    o_send, o_recv,
):
    outer, inner, head = (lax.axis_index(a) for a in ("outer", "inner", "head"))
    outers, heads = lax.axis_size("outer"), lax.axis_size("head")
    inners = lax.axis_size("inner")
    y, z = inner // ring, inner % ring
    part = q_in.shape[1] // group
    half = 2 * part
    keys = heads * part
    head_dim = q_in.shape[2]
    scale = math.log2(math.e) / math.sqrt(head_dim)
    core = outer % 2
    turn = 2 * core - 1
    after, before = (outer + 1) % outers, (outer + outers - 1) % outers
    near = jnp.where(core == 0, y, 1 - y)

    def at_head(by):
        return (outer, inner, (head + by) % heads)

    def at_next(y_there):
        return (after, y_there * ring + z, head)

    def at_z(by):
        return (outer, y * ring + (z + by + ring) % ring, head)

    y_peer = (outer, (1 - y) * ring + z, head)

    barrier = pltpu.get_barrier_semaphore()
    peers = [at_head(r) for r in (1, 2, 3)]
    peers += [at_next(0), at_next(1), (before, z, head), (before, ring + z, head)]
    peers += [at_z(1), at_z(-1), y_peer]
    for peer in peers:
        pl.semaphore_signal(barrier, inc=1, device_id=peer, device_id_type=MESH)
    pl.semaphore_wait(barrier, len(peers))

    def remote(src, dst, send, recv, peer):
        return pltpu.make_async_remote_copy(
            src_ref=src, dst_ref=dst, send_sem=send, recv_sem=recv,
            device_id=peer, device_id_type=MESH,
        )

    def kv_copy(r):
        there = (head + r) % heads
        return remote(kv_in.at[there], own.at[:, head], x_send.at[r], x_recv.at[r], at_head(r))

    def q_copy(r):
        there = (head + r) % heads
        return remote(q_in.at[there], qbuf.at[heads - r], q_send.at[r], q_recv.at[r], at_head(r))

    for r in (1, 3, 2):
        kv_copy(r).start()
    for r in (1, 3, 2):
        q_copy(r).start()

    def first_copy(r, n):
        p = (head + r) % heads
        src, dst, y_there = (
            (own.at[1, p], vbuf.at[0, z, p], near),
            (own.at[0, p], kbuf.at[0, z, p], near),
            (own.at[0, p], kbuf.at[1, z, p], 1 - near),
        )[n]
        return remote(src, dst, first_send.at[n, r], first_recv.at[n, p], at_next(y_there))

    def send_first(r):
        if r:
            kv_copy(heads - r).wait_recv()
        for n in range(3):
            first_copy(r, n).start()

    def k_copy(way, kind, origin):
        peer = at_z(turn if way == 0 else -turn)
        return remote(
            kbuf.at[kind, origin], kbuf.at[kind, origin],
            k_send.at[way, kind, origin], k_recv.at[kind, origin], peer,
        )

    def v_copy(way, origin):
        peer = at_z(turn if way == 0 else -turn)
        return remote(
            vbuf.at[0, origin], vbuf.at[0, origin],
            v_send.at[way, origin], v_recv.at[0, origin], peer,
        )

    def y_copy(origin):
        return remote(
            vbuf.at[0, origin], vbuf.at[1, origin], y_send.at[origin], v_recv.at[1, origin], y_peer
        )

    def origin_of(way, step):
        by = turn * step
        return (z - by + ring) % ring if way == 0 else (z + by + ring) % ring

    def pass_first(r, ns):
        p = (head + r) % heads
        for n in ns:
            first_copy(r, n).wait_recv()
            for way in (0, 1):
                peer = at_z(turn if way == 0 else -turn)
                if n == 0:
                    buf, send, recv = vbuf.at[0, z, p], v_send.at[way, z], v_recv.at[0, z]
                else:
                    buf = kbuf.at[n - 1, z, p]
                    send, recv = k_send.at[way, n - 1, z], k_recv.at[n - 1, z]
                remote(buf, buf, send, recv, peer).start()

    def last_step(way, kind):
        return ring // 2 if way == kind else ring // 2 - 1

    def v_event(way, step):
        origin = origin_of(way, step)
        v_copy(way, origin).wait_recv()
        pl.when(step < last_step(way, 0))(lambda: v_copy(way, origin).start())
        y_copy(origin).start()

    def k_event(way, kind, step):
        origin = origin_of(way, step)
        k_copy(way, kind, origin).wait_recv()
        pl.when(step < last_step(way, kind))(lambda: k_copy(way, kind, origin).start())

    def k_events(kind, step):
        k_event(0, kind, step)
        k_event(1, kind, step)

    def y_event(origin):
        remote(
            vbuf.at[1, origin], vbuf.at[1, origin], y_send.at[origin], v_recv.at[1, origin], y_peer
        ).wait_recv()

    def slot_of(c):
        step, place = c // 4, c % 4
        kind = jnp.where(step == 0, place - 2, jnp.where(step == ring // 2, place, place // 2))
        sign = 1 - 2 * (place % 2)
        return kind, (z - turn * sign * step + ring) % ring

    def halves_of(c):
        kind, origin = slot_of(c)
        y_there = jnp.where((core + kind) % 2 == 1, y, 1 - y)
        block = before * inners + y_there * ring + origin
        return order_ref[2 * block], order_ref[2 * block + 1]

    here = 2 * (outer * inners + inner)
    here_order = (order_ref[here], order_ref[here + 1])

    def tile_order(r):
        return jnp.where((head + r) % heads < 2, here_order[0], here_order[1])

    scores = (s0, s1)
    columns = group * part

    def score(k_rows, r):
        q = qbuf[r]
        return lax.dot_general(k_rows, q, NT, preferred_element_type=jnp.float32) * scale

    def ahead(c, r, slot):
        kind, origin = slot_of(c)
        for h in range(2):
            k_rows = kbuf[kind, origin, 2 * h : 2 * h + 2].reshape(half, head_dim)
            s = score(k_rows, r)
            scores[slot][h * half : (h + 1) * half] = s
            tile_max[slot, h] = jnp.max(s, axis=0, keepdims=True)

    def ahead_own(r, slot):
        token = lax.broadcasted_iota(jnp.int32, (1, columns), 1) % part
        q_token = ((head + r) % 2) * part + token
        q_pos = tile_order(r) * half + q_token
        for h in range(2):
            k_rows = own[0, 2 * h : 2 * h + 2].reshape(half, head_dim)
            k_pos = here_order[h] * half + lax.broadcasted_iota(jnp.int32, (half, 1), 0)
            s = jnp.where(k_pos <= q_pos, score(k_rows, r), NEG)
            scores[slot][h * half : (h + 1) * half] = s
            tile_max[slot, h] = jnp.max(s, axis=0, keepdims=True)

    def absorb(v_parts, hidden, r, slot, first=False):
        new = jnp.maximum(tile_max[slot, 0] - hidden[0], tile_max[slot, 1] - hidden[1])
        if not first:
            old = m_ref[r]
            new = jnp.maximum(old, new)
            shrink = jnp.exp2(old - new)
        m_ref[r] = new
        weights = jnp.concatenate(
            [
                jnp.exp2(scores[slot][h * half : (h + 1) * half] - (new + hidden[h]))
                for h in range(2)
            ],
            axis=0,
        ).astype(jnp.bfloat16)
        v = jnp.concatenate(v_parts, axis=1)
        v = jnp.concatenate([v, jnp.ones((16, keys), jnp.bfloat16)], axis=0)
        add = lax.dot_general(v, weights, NN, preferred_element_type=jnp.float32)
        add = add[: head_dim + 8]
        acc_ref[r] = add if first else acc_ref[r] * shrink + add

    def now(c, r, slot):
        kind, origin = slot_of(c)
        mine = tile_order(r)
        hidden = [jnp.where(k < mine, 0.0, -NEG) for k in halves_of(c)]
        absorb([vbuf[kind, origin, x] for x in range(heads)], hidden, r, slot)

    def now_own(r, slot):
        absorb([own[1, x] for x in range(heads)], (0.0, 0.0), r, slot, first=True)

    def out_copy(r):
        return remote(
            outbuf.at[r], out_ref.at[head], o_send.at[r], o_recv.at[r], at_head(r)
        )

    def finish(r):
        total = acc_ref[r, head_dim : head_dim + 1]
        rows = (acc_ref[r, :head_dim] / total).T.astype(jnp.bfloat16)
        there = (head + r) % heads
        if r == 0:
            out_ref[head] = rows
        else:
            outbuf[r] = rows
            out_copy(r).start()
        logs = (m_ref[r] + jnp.log2(total)) * LN2
        for g in range(group):
            log_ref[g : g + 1, pl.ds(pl.multiple_of(there * part, part), part)] = logs[
                :, g * part : (g + 1) * part
            ]

    own[0, head] = kv_in[head, 0]
    own[1, head] = kv_in[head, 1]
    send_first(0)
    qbuf[0] = q_in[head]
    send_first(ARRIVAL[1])
    pass_first(ARRIVAL[0], (0, 1))
    send_first(ARRIVAL[2])
    pass_first(ARRIVAL[1], (0, 1))
    send_first(ARRIVAL[3])
    pass_first(ARRIVAL[2], (0, 1))
    pass_first(ARRIVAL[0], (2,))
    pass_first(ARRIVAL[1], (2,))
    pass_first(ARRIVAL[3], (0, 1))
    y_copy(z).start()
    pass_first(ARRIVAL[2], (2,))
    pass_first(ARRIVAL[3], (2,))

    def do_ahead(c, r, slot):
        if c == 0:
            if r:
                q_copy(heads - r).wait_recv()
            ahead_own(r, slot)
        else:
            ahead(c, r, slot)

    early = [(0, 0), (2, 0), (0, 1), (2, 1), (0, 3), (2, 3)]
    early += [(3, 0), (3, 1), (3, 3), (0, 2), (2, 2), (3, 2)]
    do_ahead(*early[0], 0)
    for n in range(11):
        if early[n + 1] == (0, 3):
            v_event(0, 1)
            v_event(1, 1)
        if early[n + 1] == (0, 2):
            k_events(0, 1)
        do_ahead(*early[n + 1], (n + 1) % 2)
        c, r = early[n]
        if (c, r) == (3, 0):
            y_event(z)
        if c == 0:
            now_own(r, n % 2)
        else:
            now(c, r, n % 2)

    def events(c):
        step, place = c // 4, c % 4

        @pl.when(jnp.logical_and(place == 0, step > 1))
        def _():
            k_events(0, step)

        @pl.when(place == K1_PLACE)
        def _():
            k_events(1, step)

        @pl.when(place == 2)
        def _():
            y_event(origin_of(0, step))

        @pl.when(place == 3)
        def _():
            y_event(origin_of(1, step))
            v_event(0, step + 1)
            pl.when(step < 3)(lambda: v_event(1, step + 1))

    def chunk(c, _):
        events(c)
        ahead(c, LOOP[0], 0)
        now(c - 1, LOOP[3], 1)
        for n in range(3):
            ahead(c, LOOP[n + 1], (n + 1) % 2)
            now(c, LOOP[n], n % 2)
        return 0

    lax.fori_loop(4, 16, chunk, 0)
    k_event(0, 0, ring // 2)
    k_event(1, 1, ring // 2)
    y_event(origin_of(0, ring // 2))
    ahead(16, ORDER[0], 0)
    now(15, LOOP[3], 1)
    for n, r in enumerate(ORDER):
        ahead(17, r, 1)
        now(16, r, 0)
        if n < 3:
            ahead(16, ORDER[n + 1], 0)
        now(17, r, 1)
        finish(r)

    for r in (1, 2, 3):
        out_copy(r).wait_recv()
    for r in (1, 2, 3):
        out_copy(r).wait_send()
        kv_copy(r).wait_send()
        q_copy(r).wait_send()
    for r in range(heads):
        for n in range(3):
            first_copy(r, n).wait_send()
    y_copy(z).wait_send()
    for way in (0, 1):
        v_copy(way, z).wait_send()
        for kind in (0, 1):
            k_copy(way, kind, z).wait_send()

    def ended(step, _):
        for way in (0, 1):
            origin = origin_of(way, step)
            y_copy(origin).wait_send()
            pl.when(step < last_step(way, 0))(lambda: v_copy(way, origin).wait_send())
            for kind in (0, 1):
                pl.when(step < last_step(way, kind))(
                    lambda: k_copy(way, kind, origin).wait_send()
                )
        return 0

    lax.fori_loop(1, 4, ended, 0)
    y_copy(origin_of(0, ring // 2)).wait_send()


def body(queries, keys, values, block_order):
    heads = lax.axis_size("head")
    inners = lax.axis_size("inner")
    part, q_heads, head_dim = queries.shape
    group = q_heads // heads
    ring = inners // 2
    columns = group * part
    q_in = jnp.transpose(queries, (1, 0, 2)).reshape(heads, columns, head_dim)
    kv_in = jnp.stack([jnp.transpose(keys, (1, 0, 2)), jnp.transpose(values, (1, 2, 0))], axis=1)
    block = heads * part
    bf16, f32 = jnp.bfloat16, jnp.float32
    dma = pltpu.SemaphoreType.DMA
    vmem = pl.BlockSpec(memory_space=pltpu.VMEM)
    rows, logs = pl.pallas_call(
        functools.partial(kernel, group, ring),
        out_shape=(
            jax.ShapeDtypeStruct((heads, columns, head_dim), bf16),
            jax.ShapeDtypeStruct((group, block), f32),
        ),
        in_specs=[pl.BlockSpec(memory_space=pltpu.SMEM), vmem, vmem],
        out_specs=(vmem, vmem),
        scratch_shapes=[
            pltpu.VMEM((heads, columns, head_dim), bf16),
            pltpu.VMEM((2, heads, part, head_dim), bf16),
            pltpu.VMEM((2, ring, heads, part, head_dim), bf16),
            pltpu.VMEM((2, ring, heads, head_dim, part), bf16),
            pltpu.VMEM((heads, columns, head_dim), bf16),
            pltpu.VMEM((heads, 1, columns), f32),
            pltpu.VMEM((heads, head_dim + 8, columns), f32),
            pltpu.VMEM((block, columns), f32),
            pltpu.VMEM((block, columns), f32),
            pltpu.VMEM((2, 2, 1, columns), f32),
            dma((heads,)),
            dma((heads,)),
            dma((heads,)),
            dma((heads,)),
            dma((3, heads)),
            dma((3, heads)),
            dma((2, ring)),
            dma((2, ring)),
            dma((2, 2, ring)),
            dma((2, ring)),
            dma((ring,)),
            dma((heads,)),
            dma((heads,)),
        ],
        compiler_params=pltpu.CompilerParams(
            collective_id=0, has_side_effects=True, vmem_limit_bytes=48 * 2**20
        ),
        cost_estimate=pl.CostEstimate(
            flops=4 * q_heads * block * (2 * ring + 1) * block * head_dim // heads,
            bytes_accessed=4 * 2**20,
            transcendentals=q_heads * block * (2 * ring + 1) * block // heads,
        ),
    )(block_order, q_in, kv_in)
    attended = jnp.transpose(rows.reshape(q_heads, part, head_dim), (1, 0, 2))
    return attended, logs


def solution(mesh):
    spread = P(("outer", "inner", "head"), None, None)
    return jax.shard_map(
        body,
        mesh=mesh,
        in_specs=(spread, spread, spread, P()),
        out_specs=(spread, P("head", ("outer", "inner"))),
        check_vma=False,
    )
```

```python
import functools
import math

import jax
import jax.numpy as jnp
from jax import lax
from jax.experimental import pallas as pl
from jax.experimental.pallas import tpu as pltpu
from jax.sharding import PartitionSpec as P

MESH = pl.DeviceIdType.MESH
NEG = -1e30
LN2 = math.log(2.0)
NT = (((1,), (1,)), ((), ()))
NN = (((1,), (0,)), ((), ()))
ARRIVAL = (0, 1, 3, 2)
LOOP = (1, 3, 0, 2)
ORDER = (2, 1, 3, 0)
K1_PLACE = 1


def kernel(
    group, ring, order_in, q_hbm, k_hbm, v_hbm, out_ref, log_ref,
    order_ref, q_ref, k_ref, v_ref, q_in, kv_in, got, qbuf, own, kbuf, vbuf, outbuf, m_ref, acc_ref, s0, s1, tile_max,
    q_send, q_recv, x_send, x_recv, first_send, first_recv, k_recv, v_recv, k_send, v_send, y_send,
    o_send, o_recv, in_sem,
):
    outer, inner, head = (lax.axis_index(a) for a in ("outer", "inner", "head"))
    outers, heads = lax.axis_size("outer"), lax.axis_size("head")
    inners = lax.axis_size("inner")
    y, z = inner // ring, inner % ring
    part = q_in.shape[1] // group
    half = 2 * part
    keys = heads * part
    head_dim = q_in.shape[2]
    scale = math.log2(math.e) / math.sqrt(head_dim)
    core = outer % 2
    turn = 2 * core - 1
    after, before = (outer + 1) % outers, (outer + outers - 1) % outers
    near = jnp.where(core == 0, y, 1 - y)

    def at_head(by):
        return (outer, inner, (head + by) % heads)

    def at_next(y_there):
        return (after, y_there * ring + z, head)

    def at_z(by):
        return (outer, y * ring + (z + by + ring) % ring, head)

    y_peer = (outer, (1 - y) * ring + z, head)
    loads = [
        pltpu.make_async_copy(src, dst, in_sem.at[n])
        for n, (src, dst) in enumerate(
            ((k_hbm, k_ref), (v_hbm, v_ref), (q_hbm, q_ref), (order_in, order_ref))
        )
    ]
    for load in loads:
        load.start()

    barrier = pltpu.get_barrier_semaphore()
    peers = [at_head(r) for r in (1, 2, 3)]
    peers += [at_next(0), at_next(1), (before, z, head), (before, ring + z, head)]
    peers += [at_z(1), at_z(-1), y_peer]
    for peer in peers:
        pl.semaphore_signal(barrier, inc=1, device_id=peer, device_id_type=MESH)
    loads[0].wait()
    loads[1].wait()
    kv_in[:, 0] = jnp.swapaxes(k_ref[...], 0, 1)
    v_rows = jnp.swapaxes(v_ref[...], 0, 1)
    for x in range(heads):
        kv_in[x, 1] = v_rows[x].T
    pl.semaphore_wait(barrier, len(peers))

    def remote(src, dst, send, recv, peer):
        return pltpu.make_async_remote_copy(
            src_ref=src, dst_ref=dst, send_sem=send, recv_sem=recv,
            device_id=peer, device_id_type=MESH,
        )

    def kv_copy(r):
        there = (head + r) % heads
        return remote(kv_in.at[there], own.at[:, head], x_send.at[r], x_recv.at[r], at_head(r))

    def q_copy(r):
        there = (head + r) % heads
        return remote(q_in.at[there], qbuf.at[heads - r], q_send.at[r], q_recv.at[r], at_head(r))

    for r in (1, 3, 2):
        kv_copy(r).start()
    loads[2].wait()
    q_in[...] = jnp.swapaxes(q_ref[...], 0, 1).reshape(q_in.shape)
    for r in (1, 3, 2):
        q_copy(r).start()
    loads[3].wait()

    def first_copy(r, n):
        p = (head + r) % heads
        src, dst, y_there = (
            (own.at[1, p], vbuf.at[0, z, p], near),
            (own.at[0, p], kbuf.at[0, z, p], near),
            (own.at[0, p], kbuf.at[1, z, p], 1 - near),
        )[n]
        return remote(src, dst, first_send.at[n, r], first_recv.at[n, p], at_next(y_there))

    def send_first(r):
        if r:
            kv_copy(heads - r).wait_recv()
        for n in range(3):
            first_copy(r, n).start()

    def k_copy(way, kind, origin):
        peer = at_z(turn if way == 0 else -turn)
        return remote(
            kbuf.at[kind, origin], kbuf.at[kind, origin],
            k_send.at[way, kind, origin], k_recv.at[kind, origin], peer,
        )

    def v_copy(way, origin):
        peer = at_z(turn if way == 0 else -turn)
        return remote(
            vbuf.at[0, origin], vbuf.at[0, origin],
            v_send.at[way, origin], v_recv.at[0, origin], peer,
        )

    def y_copy(origin):
        return remote(
            vbuf.at[0, origin], vbuf.at[1, origin], y_send.at[origin], v_recv.at[1, origin], y_peer
        )

    def origin_of(way, step):
        by = turn * step
        return (z - by + ring) % ring if way == 0 else (z + by + ring) % ring

    def pass_first(r, ns):
        p = (head + r) % heads
        for n in ns:
            first_copy(r, n).wait_recv()
            for way in (0, 1):
                peer = at_z(turn if way == 0 else -turn)
                if n == 0:
                    buf, send, recv = vbuf.at[0, z, p], v_send.at[way, z], v_recv.at[0, z]
                else:
                    buf = kbuf.at[n - 1, z, p]
                    send, recv = k_send.at[way, n - 1, z], k_recv.at[n - 1, z]
                remote(buf, buf, send, recv, peer).start()

    def last_step(way, kind):
        return ring // 2 if way == kind else ring // 2 - 1

    def v_event(way, step):
        origin = origin_of(way, step)
        v_copy(way, origin).wait_recv()
        pl.when(step < last_step(way, 0))(lambda: v_copy(way, origin).start())
        y_copy(origin).start()

    def k_event(way, kind, step):
        origin = origin_of(way, step)
        k_copy(way, kind, origin).wait_recv()
        pl.when(step < last_step(way, kind))(lambda: k_copy(way, kind, origin).start())

    def k_events(kind, step):
        k_event(0, kind, step)
        k_event(1, kind, step)

    def y_event(origin):
        remote(
            vbuf.at[1, origin], vbuf.at[1, origin], y_send.at[origin], v_recv.at[1, origin], y_peer
        ).wait_recv()

    def slot_of(c):
        step, place = c // 4, c % 4
        kind = jnp.where(step == 0, place - 2, jnp.where(step == ring // 2, place, place // 2))
        sign = 1 - 2 * (place % 2)
        return kind, (z - turn * sign * step + ring) % ring

    def halves_of(c):
        kind, origin = slot_of(c)
        y_there = jnp.where((core + kind) % 2 == 1, y, 1 - y)
        block = before * inners + y_there * ring + origin
        return order_ref[2 * block], order_ref[2 * block + 1]

    here = 2 * (outer * inners + inner)
    here_order = (order_ref[here], order_ref[here + 1])

    def tile_order(r):
        return jnp.where((head + r) % heads < 2, here_order[0], here_order[1])

    scores = (s0, s1)
    columns = group * part

    def score(k_rows, r):
        q = qbuf[r]
        return lax.dot_general(k_rows, q, NT, preferred_element_type=jnp.float32) * scale

    def ahead(c, r, slot):
        kind, origin = slot_of(c)
        for h in range(2):
            k_rows = kbuf[kind, origin, 2 * h : 2 * h + 2].reshape(half, head_dim)
            s = score(k_rows, r)
            scores[slot][h * half : (h + 1) * half] = s
            tile_max[slot, h] = jnp.max(s, axis=0, keepdims=True)

    def ahead_own(r, slot):
        token = lax.broadcasted_iota(jnp.int32, (1, columns), 1) % part
        q_token = ((head + r) % 2) * part + token
        q_pos = tile_order(r) * half + q_token
        for h in range(2):
            k_rows = own[0, 2 * h : 2 * h + 2].reshape(half, head_dim)
            k_pos = here_order[h] * half + lax.broadcasted_iota(jnp.int32, (half, 1), 0)
            s = jnp.where(k_pos <= q_pos, score(k_rows, r), NEG)
            scores[slot][h * half : (h + 1) * half] = s
            tile_max[slot, h] = jnp.max(s, axis=0, keepdims=True)

    def absorb(v_parts, hidden, r, slot, first=False):
        new = jnp.maximum(tile_max[slot, 0] - hidden[0], tile_max[slot, 1] - hidden[1])
        if not first:
            old = m_ref[r]
            new = jnp.maximum(old, new)
            shrink = jnp.exp2(old - new)
        m_ref[r] = new
        weights = jnp.concatenate(
            [
                jnp.exp2(scores[slot][h * half : (h + 1) * half] - (new + hidden[h]))
                for h in range(2)
            ],
            axis=0,
        ).astype(jnp.bfloat16)
        v = jnp.concatenate(v_parts, axis=1)
        v = jnp.concatenate([v, jnp.ones((16, keys), jnp.bfloat16)], axis=0)
        add = lax.dot_general(v, weights, NN, preferred_element_type=jnp.float32)
        add = add[: head_dim + 8]
        acc_ref[r] = add if first else acc_ref[r] * shrink + add

    def now(c, r, slot):
        kind, origin = slot_of(c)
        mine = tile_order(r)
        hidden = [jnp.where(k < mine, 0.0, -NEG) for k in halves_of(c)]
        absorb([vbuf[kind, origin, x] for x in range(heads)], hidden, r, slot)

    def now_own(r, slot):
        absorb([own[1, x] for x in range(heads)], (0.0, 0.0), r, slot, first=True)

    def out_copy(r):
        return remote(
            outbuf.at[r], got.at[head], o_send.at[r], o_recv.at[r], at_head(r)
        )

    def finish(r):
        total = acc_ref[r, head_dim : head_dim + 1]
        rows = (acc_ref[r, :head_dim] / total).T.astype(jnp.bfloat16)
        there = (head + r) % heads
        if r == 0:
            got[head] = rows
        else:
            outbuf[r] = rows
            out_copy(r).start()
        logs = (m_ref[r] + jnp.log2(total)) * LN2
        for g in range(group):
            log_ref[g : g + 1, pl.ds(pl.multiple_of(there * part, part), part)] = logs[
                :, g * part : (g + 1) * part
            ]

    own[0, head] = kv_in[head, 0]
    own[1, head] = kv_in[head, 1]
    send_first(0)
    qbuf[0] = q_in[head]
    send_first(ARRIVAL[1])
    pass_first(ARRIVAL[0], (0, 1))
    send_first(ARRIVAL[2])
    pass_first(ARRIVAL[1], (0, 1))
    send_first(ARRIVAL[3])
    pass_first(ARRIVAL[2], (0, 1))
    pass_first(ARRIVAL[0], (2,))
    pass_first(ARRIVAL[1], (2,))
    pass_first(ARRIVAL[3], (0, 1))
    y_copy(z).start()
    pass_first(ARRIVAL[2], (2,))
    pass_first(ARRIVAL[3], (2,))

    def do_ahead(c, r, slot):
        if c == 0:
            if r:
                q_copy(heads - r).wait_recv()
            ahead_own(r, slot)
        else:
            ahead(c, r, slot)

    early = [(0, 0), (2, 0), (0, 1), (2, 1), (0, 3), (2, 3)]
    early += [(3, 0), (3, 1), (3, 3), (0, 2), (2, 2), (3, 2)]
    do_ahead(*early[0], 0)
    for n in range(11):
        if early[n + 1] == (0, 3):
            v_event(0, 1)
            v_event(1, 1)
        if early[n + 1] == (0, 2):
            k_events(0, 1)
        do_ahead(*early[n + 1], (n + 1) % 2)
        c, r = early[n]
        if (c, r) == (3, 0):
            y_event(z)
        if c == 0:
            now_own(r, n % 2)
        else:
            now(c, r, n % 2)

    def events(c):
        step, place = c // 4, c % 4

        @pl.when(jnp.logical_and(place == 0, step > 1))
        def _():
            k_events(0, step)

        @pl.when(place == K1_PLACE)
        def _():
            k_events(1, step)

        @pl.when(place == 2)
        def _():
            y_event(origin_of(0, step))

        @pl.when(place == 3)
        def _():
            y_event(origin_of(1, step))
            v_event(0, step + 1)
            pl.when(step < 3)(lambda: v_event(1, step + 1))

    def chunk(c, _):
        events(c)
        ahead(c, LOOP[0], 0)
        now(c - 1, LOOP[3], 1)
        for n in range(3):
            ahead(c, LOOP[n + 1], (n + 1) % 2)
            now(c, LOOP[n], n % 2)
        return 0

    lax.fori_loop(4, 16, chunk, 0)
    k_event(0, 0, ring // 2)
    k_event(1, 1, ring // 2)
    y_event(origin_of(0, ring // 2))
    ahead(16, ORDER[0], 0)
    now(15, LOOP[3], 1)
    for n, r in enumerate(ORDER):
        ahead(17, r, 1)
        now(16, r, 0)
        if n < 3:
            ahead(16, ORDER[n + 1], 0)
        now(17, r, 1)
        finish(r)

    for r in (1, 2, 3):
        out_copy(r).wait_recv()
    out_ref[...] = jnp.swapaxes(got[...].reshape(heads * group, part, head_dim), 0, 1)
    for r in (1, 2, 3):
        out_copy(r).wait_send()
        kv_copy(r).wait_send()
        q_copy(r).wait_send()
    for r in range(heads):
        for n in range(3):
            first_copy(r, n).wait_send()
    y_copy(z).wait_send()
    for way in (0, 1):
        v_copy(way, z).wait_send()
        for kind in (0, 1):
            k_copy(way, kind, z).wait_send()

    def ended(step, _):
        for way in (0, 1):
            origin = origin_of(way, step)
            y_copy(origin).wait_send()
            pl.when(step < last_step(way, 0))(lambda: v_copy(way, origin).wait_send())
            for kind in (0, 1):
                pl.when(step < last_step(way, kind))(
                    lambda: k_copy(way, kind, origin).wait_send()
                )
        return 0

    lax.fori_loop(1, 4, ended, 0)
    y_copy(origin_of(0, ring // 2)).wait_send()


def body(queries, keys, values, block_order):
    heads = lax.axis_size("head")
    inners = lax.axis_size("inner")
    part, q_heads, head_dim = queries.shape
    group = q_heads // heads
    ring = inners // 2
    columns = group * part
    block = heads * part
    bf16, f32 = jnp.bfloat16, jnp.float32
    dma = pltpu.SemaphoreType.DMA
    vmem = pl.BlockSpec(memory_space=pltpu.VMEM)
    return pl.pallas_call(
        functools.partial(kernel, group, ring),
        out_shape=(
            jax.ShapeDtypeStruct(queries.shape, bf16),
            jax.ShapeDtypeStruct((group, block), f32),
        ),
        in_specs=[pl.BlockSpec(memory_space=pltpu.HBM)] * 4,
        out_specs=(vmem, vmem),
        scratch_shapes=[
            pltpu.SMEM(block_order.shape, jnp.int32),
            pltpu.VMEM(queries.shape, bf16),
            pltpu.VMEM(keys.shape, bf16),
            pltpu.VMEM(values.shape, bf16),
            pltpu.VMEM((heads, columns, head_dim), bf16),
            pltpu.VMEM((heads, 2, part, head_dim), bf16),
            pltpu.VMEM((heads, columns, head_dim), bf16),
            pltpu.VMEM((heads, columns, head_dim), bf16),
            pltpu.VMEM((2, heads, part, head_dim), bf16),
            pltpu.VMEM((2, ring, heads, part, head_dim), bf16),
            pltpu.VMEM((2, ring, heads, head_dim, part), bf16),
            pltpu.VMEM((heads, columns, head_dim), bf16),
            pltpu.VMEM((heads, 1, columns), f32),
            pltpu.VMEM((heads, head_dim + 8, columns), f32),
            pltpu.VMEM((block, columns), f32),
            pltpu.VMEM((block, columns), f32),
            pltpu.VMEM((2, 2, 1, columns), f32),
            dma((heads,)),
            dma((heads,)),
            dma((heads,)),
            dma((heads,)),
            dma((3, heads)),
            dma((3, heads)),
            dma((2, ring)),
            dma((2, ring)),
            dma((2, 2, ring)),
            dma((2, ring)),
            dma((ring,)),
            dma((heads,)),
            dma((heads,)),
            dma((4,)),
        ],
        compiler_params=pltpu.CompilerParams(
            collective_id=0, has_side_effects=True, vmem_limit_bytes=60 * 2**20
        ),
        cost_estimate=pl.CostEstimate(
            flops=4 * q_heads * block * (2 * ring + 1) * block * head_dim // heads,
            bytes_accessed=4 * 2**20,
            transcendentals=q_heads * block * (2 * ring + 1) * block // heads,
        ),
    )(block_order, queries, keys, values)


def solution(mesh):
    spread = P(("outer", "inner", "head"), None, None)
    return jax.shard_map(
        body,
        mesh=mesh,
        in_specs=(spread, spread, spread, P()),
        out_specs=(spread, P("head", ("outer", "inner"))),
        check_vma=False,
    )
```

```python
import functools
import math

import jax
import jax.numpy as jnp
from jax import lax
from jax.experimental import pallas as pl
from jax.experimental.pallas import tpu as pltpu
from jax.sharding import PartitionSpec as P

MESH = pl.DeviceIdType.MESH
NEG = -1e30
LN2 = math.log(2.0)
NT = (((1,), (1,)), ((), ()))
NN = (((1,), (0,)), ((), ()))
ARRIVAL = (0, 1, 3, 2)
LOOP = (1, 3, 0, 2)
ORDER = (2, 1, 3, 0)
LAST = 16
K1_PLACE = 1


def kernel(
    group, ring, order_in, q_hbm, k_hbm, v_hbm, out_ref, log_ref,
    order_ref, q_ref, k_ref, v_ref, q_in, kv_in, got, qbuf, own, kbuf, vbuf, outbuf, m_ref, acc_ref, s0, s1, tile_max,
    q_send, q_recv, x_send, x_recv, first_send, first_recv, k_recv, v_recv, k_send, v_send, y_send,
    o_send, o_recv, in_sem,
):
    outer, inner, head = (lax.axis_index(a) for a in ("outer", "inner", "head"))
    outers, heads = lax.axis_size("outer"), lax.axis_size("head")
    inners = lax.axis_size("inner")
    y, z = inner // ring, inner % ring
    part = q_in.shape[1] // group
    half = 2 * part
    keys = heads * part
    head_dim = q_in.shape[2]
    scale = math.log2(math.e) / math.sqrt(head_dim)
    core = outer % 2
    turn = 2 * core - 1
    after, before = (outer + 1) % outers, (outer + outers - 1) % outers
    near = jnp.where(core == 0, y, 1 - y)

    def at_head(by):
        return (outer, inner, (head + by) % heads)

    def at_next(y_there):
        return (after, y_there * ring + z, head)

    def at_z(by):
        return (outer, y * ring + (z + by + ring) % ring, head)

    y_peer = (outer, (1 - y) * ring + z, head)
    loads = [
        pltpu.make_async_copy(src, dst, in_sem.at[n])
        for n, (src, dst) in enumerate(
            ((k_hbm, k_ref), (v_hbm, v_ref), (q_hbm, q_ref), (order_in, order_ref))
        )
    ]
    for load in loads:
        load.start()

    barrier = pltpu.get_barrier_semaphore()
    peers = [at_head(r) for r in (1, 2, 3)]
    peers += [at_next(0), at_next(1), (before, z, head), (before, ring + z, head)]
    peers += [at_z(1), at_z(-1), y_peer]
    for peer in peers:
        pl.semaphore_signal(barrier, inc=1, device_id=peer, device_id_type=MESH)
    loads[0].wait()
    loads[1].wait()
    kv_in[:, 0] = jnp.swapaxes(k_ref[...], 0, 1)
    v_rows = jnp.swapaxes(v_ref[...], 0, 1)
    for x in range(heads):
        kv_in[x, 1] = v_rows[x].T
    pl.semaphore_wait(barrier, len(peers))

    def remote(src, dst, send, recv, peer):
        return pltpu.make_async_remote_copy(
            src_ref=src, dst_ref=dst, send_sem=send, recv_sem=recv,
            device_id=peer, device_id_type=MESH,
        )

    def kv_copy(r):
        there = (head + r) % heads
        return remote(kv_in.at[there], own.at[:, head], x_send.at[r], x_recv.at[r], at_head(r))

    def q_copy(r):
        there = (head + r) % heads
        return remote(q_in.at[there], qbuf.at[heads - r], q_send.at[r], q_recv.at[r], at_head(r))

    for r in (1, 3, 2):
        kv_copy(r).start()
    loads[2].wait()
    q_in[...] = jnp.swapaxes(q_ref[...], 0, 1).reshape(q_in.shape)
    for r in (1, 3, 2):
        q_copy(r).start()
    loads[3].wait()

    def first_copy(r, n):
        p = (head + r) % heads
        src, dst, y_there = (
            (own.at[1, p], vbuf.at[0, z, p], near),
            (own.at[0, p], kbuf.at[0, z, p], near),
            (own.at[0, p], kbuf.at[1, z, p], 1 - near),
        )[n]
        return remote(src, dst, first_send.at[n, r], first_recv.at[n, p], at_next(y_there))

    def send_first(r):
        if r:
            kv_copy(heads - r).wait_recv()
        for n in range(3):
            first_copy(r, n).start()

    def k_copy(way, kind, origin):
        peer = at_z(turn if way == 0 else -turn)
        return remote(
            kbuf.at[kind, origin], kbuf.at[kind, origin],
            k_send.at[way, kind, origin], k_recv.at[kind, origin], peer,
        )

    def v_copy(way, origin):
        peer = at_z(turn if way == 0 else -turn)
        return remote(
            vbuf.at[0, origin], vbuf.at[0, origin],
            v_send.at[way, origin], v_recv.at[0, origin], peer,
        )

    def y_copy(origin):
        return remote(
            vbuf.at[0, origin], vbuf.at[1, origin], y_send.at[origin], v_recv.at[1, origin], y_peer
        )

    def origin_of(way, step):
        by = turn * step
        return (z - by + ring) % ring if way == 0 else (z + by + ring) % ring

    def pass_first(r, ns):
        p = (head + r) % heads
        for n in ns:
            first_copy(r, n).wait_recv()
            for way in (0, 1):
                peer = at_z(turn if way == 0 else -turn)
                if n == 0:
                    buf, send, recv = vbuf.at[0, z, p], v_send.at[way, z], v_recv.at[0, z]
                else:
                    buf = kbuf.at[n - 1, z, p]
                    send, recv = k_send.at[way, n - 1, z], k_recv.at[n - 1, z]
                remote(buf, buf, send, recv, peer).start()

    def last_step(way, kind):
        return ring // 2 if way == kind else ring // 2 - 1

    def v_event(way, step):
        origin = origin_of(way, step)
        v_copy(way, origin).wait_recv()
        pl.when(step < last_step(way, 0))(lambda: v_copy(way, origin).start())
        y_copy(origin).start()

    def k_event(way, kind, step):
        origin = origin_of(way, step)
        k_copy(way, kind, origin).wait_recv()
        pl.when(step < last_step(way, kind))(lambda: k_copy(way, kind, origin).start())

    def k_events(kind, step):
        k_event(0, kind, step)
        k_event(1, kind, step)

    def y_event(origin):
        remote(
            vbuf.at[1, origin], vbuf.at[1, origin], y_send.at[origin], v_recv.at[1, origin], y_peer
        ).wait_recv()

    def slot_of(c):
        step, place = c // 4, c % 4
        kind = jnp.where(step == 0, place - 2, jnp.where(step == ring // 2, place, place // 2))
        sign = 1 - 2 * (place % 2)
        return kind, (z - turn * sign * step + ring) % ring

    def halves_of(c):
        kind, origin = slot_of(c)
        y_there = jnp.where((core + kind) % 2 == 1, y, 1 - y)
        block = before * inners + y_there * ring + origin
        return order_ref[2 * block], order_ref[2 * block + 1]

    here = 2 * (outer * inners + inner)
    here_order = (order_ref[here], order_ref[here + 1])

    def tile_order(r):
        return jnp.where((head + r) % heads < 2, here_order[0], here_order[1])

    scores = (s0, s1)
    columns = group * part

    def score(k_rows, r):
        q = qbuf[r]
        return lax.dot_general(k_rows, q, NT, preferred_element_type=jnp.float32) * scale

    def ahead(c, r, slot):
        kind, origin = slot_of(c)
        for h in range(2):
            k_rows = kbuf[kind, origin, 2 * h : 2 * h + 2].reshape(half, head_dim)
            s = score(k_rows, r)
            scores[slot][h * half : (h + 1) * half] = s
            tile_max[slot, h] = jnp.max(s, axis=0, keepdims=True)

    def ahead_own(r, slot):
        token = lax.broadcasted_iota(jnp.int32, (1, columns), 1) % part
        q_token = ((head + r) % 2) * part + token
        q_pos = tile_order(r) * half + q_token
        for h in range(2):
            k_rows = own[0, 2 * h : 2 * h + 2].reshape(half, head_dim)
            k_pos = here_order[h] * half + lax.broadcasted_iota(jnp.int32, (half, 1), 0)
            s = jnp.where(k_pos <= q_pos, score(k_rows, r), NEG)
            scores[slot][h * half : (h + 1) * half] = s
            tile_max[slot, h] = jnp.max(s, axis=0, keepdims=True)

    def absorb(v_parts, hidden, r, slot, first=False):
        new = jnp.maximum(tile_max[slot, 0] - hidden[0], tile_max[slot, 1] - hidden[1])
        if not first:
            old = m_ref[r]
            new = jnp.maximum(old, new)
            shrink = jnp.exp2(old - new)
        m_ref[r] = new
        weights = jnp.concatenate(
            [
                jnp.exp2(scores[slot][h * half : (h + 1) * half] - (new + hidden[h]))
                for h in range(2)
            ],
            axis=0,
        ).astype(jnp.bfloat16)
        v = jnp.concatenate(v_parts, axis=1)
        v = jnp.concatenate([v, jnp.ones((16, keys), jnp.bfloat16)], axis=0)
        add = lax.dot_general(v, weights, NN, preferred_element_type=jnp.float32)
        add = add[: head_dim + 8]
        acc_ref[r] = add if first else acc_ref[r] * shrink + add

    def now(c, r, slot):
        kind, origin = slot_of(c)
        mine = tile_order(r)
        hidden = [jnp.where(k < mine, 0.0, -NEG) for k in halves_of(c)]
        absorb([vbuf[kind, origin, x] for x in range(heads)], hidden, r, slot)

    def now_own(r, slot):
        absorb([own[1, x] for x in range(heads)], (0.0, 0.0), r, slot, first=True)

    def out_copy(r):
        return remote(
            outbuf.at[r], got.at[head], o_send.at[r], o_recv.at[r], at_head(r)
        )

    def finish(r):
        total = acc_ref[r, head_dim : head_dim + 1]
        rows = (acc_ref[r, :head_dim] / total).astype(jnp.bfloat16).T
        there = (head + r) % heads
        if r == 0:
            got[head] = rows
        else:
            outbuf[r] = rows
            out_copy(r).start()
        logs = (m_ref[r] + jnp.log2(total)) * LN2
        for g in range(group):
            log_ref[g : g + 1, pl.ds(pl.multiple_of(there * part, part), part)] = logs[
                :, g * part : (g + 1) * part
            ]

    own[0, head] = kv_in[head, 0]
    own[1, head] = kv_in[head, 1]
    send_first(0)
    qbuf[0] = q_in[head]
    send_first(ARRIVAL[1])
    pass_first(ARRIVAL[0], (0, 1))
    send_first(ARRIVAL[2])
    pass_first(ARRIVAL[1], (0, 1))
    send_first(ARRIVAL[3])
    pass_first(ARRIVAL[2], (0, 1))
    pass_first(ARRIVAL[0], (2,))
    pass_first(ARRIVAL[1], (2,))
    pass_first(ARRIVAL[3], (0, 1))
    y_copy(z).start()
    pass_first(ARRIVAL[2], (2,))
    pass_first(ARRIVAL[3], (2,))

    def do_ahead(c, r, slot):
        if c == 0:
            if r:
                q_copy(heads - r).wait_recv()
            ahead_own(r, slot)
        else:
            ahead(c, r, slot)

    early = [(0, 0), (2, 0), (0, 1), (2, 1), (0, 3), (2, 3)]
    early += [(3, 0), (3, 1), (3, 3), (0, 2), (2, 2), (3, 2)]
    do_ahead(*early[0], 0)
    for n in range(11):
        if early[n + 1] == (0, 3):
            v_event(0, 1)
            v_event(1, 1)
        if early[n + 1] == (0, 2):
            k_events(0, 1)
        do_ahead(*early[n + 1], (n + 1) % 2)
        c, r = early[n]
        if (c, r) == (3, 0):
            y_event(z)
        if c == 0:
            now_own(r, n % 2)
        else:
            now(c, r, n % 2)

    def events(c):
        step, place = c // 4, c % 4

        @pl.when(jnp.logical_and(place == 0, step > 1))
        def _():
            k_events(0, step)

        @pl.when(place == K1_PLACE)
        def _():
            k_events(1, step)

        @pl.when(place == 2)
        def _():
            y_event(origin_of(0, step))

        @pl.when(place == 3)
        def _():
            y_event(origin_of(1, step))
            v_event(0, step + 1)
            pl.when(step < 3)(lambda: v_event(1, step + 1))

    def chunk(c, _):
        events(c)
        ahead(c, LOOP[0], 0)
        now(c - 1, LOOP[3], 1)
        for n in range(3):
            ahead(c, LOOP[n + 1], (n + 1) % 2)
            now(c, LOOP[n], n % 2)
        return 0

    lax.fori_loop(4, LAST, chunk, 0)

    if LAST < 15:
        y_event(origin_of(0, 3))
    if LAST < 16:
        y_event(origin_of(1, 3))
        v_event(0, 4)
    steps = [(c, r) for r in ORDER for c in range(LAST, 18)]
    last = len(steps) - 1
    for n in range(-1, last + 1):
        if n < last:
            if steps[n + 1] == (16, ORDER[0]):
                k_event(0, 0, ring // 2)
            if steps[n + 1] == (17, ORDER[0]):
                k_event(1, 1, ring // 2)
            ahead(*steps[n + 1], (n + 1) % 2)
        if n < 0:
            now(LAST - 1, LOOP[3], 1)
            continue
        c, r = steps[n]
        if (c, r) == (17, ORDER[0]):
            y_event(origin_of(0, ring // 2))
        now(c, r, n % 2)
        if c == 17:
            finish(r)

    for r in (1, 2, 3):
        out_copy(r).wait_recv()
    out_ref[...] = jnp.swapaxes(got[...].reshape(heads * group, part, head_dim), 0, 1)
    for r in (1, 2, 3):
        out_copy(r).wait_send()
        kv_copy(r).wait_send()
        q_copy(r).wait_send()
    for r in range(heads):
        for n in range(3):
            first_copy(r, n).wait_send()
    y_copy(z).wait_send()
    for way in (0, 1):
        v_copy(way, z).wait_send()
        for kind in (0, 1):
            k_copy(way, kind, z).wait_send()

    def ended(step, _):
        for way in (0, 1):
            origin = origin_of(way, step)
            y_copy(origin).wait_send()
            pl.when(step < last_step(way, 0))(lambda: v_copy(way, origin).wait_send())
            for kind in (0, 1):
                pl.when(step < last_step(way, kind))(
                    lambda: k_copy(way, kind, origin).wait_send()
                )
        return 0

    lax.fori_loop(1, 4, ended, 0)
    y_copy(origin_of(0, ring // 2)).wait_send()


def body(queries, keys, values, block_order):
    heads = lax.axis_size("head")
    inners = lax.axis_size("inner")
    part, q_heads, head_dim = queries.shape
    group = q_heads // heads
    ring = inners // 2
    columns = group * part
    block = heads * part
    bf16, f32 = jnp.bfloat16, jnp.float32
    dma = pltpu.SemaphoreType.DMA
    vmem = pl.BlockSpec(memory_space=pltpu.VMEM)
    return pl.pallas_call(
        functools.partial(kernel, group, ring),
        out_shape=(
            jax.ShapeDtypeStruct(queries.shape, bf16),
            jax.ShapeDtypeStruct((group, block), f32),
        ),
        in_specs=[pl.BlockSpec(memory_space=pltpu.HBM)] * 4,
        out_specs=(vmem, vmem),
        scratch_shapes=[
            pltpu.SMEM(block_order.shape, jnp.int32),
            pltpu.VMEM(queries.shape, bf16),
            pltpu.VMEM(keys.shape, bf16),
            pltpu.VMEM(values.shape, bf16),
            pltpu.VMEM((heads, columns, head_dim), bf16),
            pltpu.VMEM((heads, 2, part, head_dim), bf16),
            pltpu.VMEM((heads, columns, head_dim), bf16),
            pltpu.VMEM((heads, columns, head_dim), bf16),
            pltpu.VMEM((2, heads, part, head_dim), bf16),
            pltpu.VMEM((2, ring, heads, part, head_dim), bf16),
            pltpu.VMEM((2, ring, heads, head_dim, part), bf16),
            pltpu.VMEM((heads, columns, head_dim), bf16),
            pltpu.VMEM((heads, 1, columns), f32),
            pltpu.VMEM((heads, head_dim + 8, columns), f32),
            pltpu.VMEM((block, columns), f32),
            pltpu.VMEM((block, columns), f32),
            pltpu.VMEM((2, 2, 1, columns), f32),
            dma((heads,)),
            dma((heads,)),
            dma((heads,)),
            dma((heads,)),
            dma((3, heads)),
            dma((3, heads)),
            dma((2, ring)),
            dma((2, ring)),
            dma((2, 2, ring)),
            dma((2, ring)),
            dma((ring,)),
            dma((heads,)),
            dma((heads,)),
            dma((4,)),
        ],
        compiler_params=pltpu.CompilerParams(
            collective_id=0, has_side_effects=True, vmem_limit_bytes=60 * 2**20
        ),
        cost_estimate=pl.CostEstimate(
            flops=4 * q_heads * block * (2 * ring + 1) * block * head_dim // heads,
            bytes_accessed=4 * 2**20,
            transcendentals=q_heads * block * (2 * ring + 1) * block // heads,
        ),
    )(block_order, queries, keys, values)


def solution(mesh):
    spread = P(("outer", "inner", "head"), None, None)
    return jax.shard_map(
        body,
        mesh=mesh,
        in_specs=(spread, spread, spread, P()),
        out_specs=(spread, P("head", ("outer", "inner"))),
        check_vma=False,
    )
```

```python
import functools
import math

import jax
import jax.numpy as jnp
from jax import lax
from jax.experimental import pallas as pl
from jax.experimental.pallas import tpu as pltpu
from jax.sharding import PartitionSpec as P

MESH = pl.DeviceIdType.MESH
NEG = -1e30
LN2 = math.log(2.0)
NT = (((1,), (1,)), ((), ()))
NN = (((1,), (0,)), ((), ()))
ARRIVAL = (0, 1, 3, 2)
LOOP = (1, 3, 0, 2)
ORDER = (2, 1, 3, 0)
LAST = 16
K1_PLACE = 1


def kernel(
    group, ring, order_in, q_hbm, k_hbm, v_hbm, out_ref, log_ref,
    order_ref, q_ref, k_ref, v_ref, q_in, kv_in, got, qbuf, own, kbuf, vbuf, outbuf, m_ref, acc_ref, s0, s1, tile_max,
    q_send, q_recv, x_send, x_recv, first_send, first_recv, k_recv, v_recv, k_send, v_send, y_send,
    o_send, o_recv, in_sem,
):
    outer, inner, head = (lax.axis_index(a) for a in ("outer", "inner", "head"))
    outers, heads = lax.axis_size("outer"), lax.axis_size("head")
    inners = lax.axis_size("inner")
    y, z = inner // ring, inner % ring
    part = q_in.shape[1] // group
    half = 2 * part
    keys = heads * part
    head_dim = q_in.shape[2]
    scale = math.log2(math.e) / math.sqrt(head_dim)
    core = outer % 2
    turn = 2 * core - 1
    after, before = (outer + 1) % outers, (outer + outers - 1) % outers
    near = jnp.where(core == 0, y, 1 - y)

    def at_head(by):
        return (outer, inner, (head + by) % heads)

    def at_next(y_there):
        return (after, y_there * ring + z, head)

    def at_z(by):
        return (outer, y * ring + (z + by + ring) % ring, head)

    y_peer = (outer, (1 - y) * ring + z, head)
    loads = [
        pltpu.make_async_copy(src, dst, in_sem.at[n])
        for n, (src, dst) in enumerate(
            ((k_hbm, k_ref), (v_hbm, v_ref), (q_hbm, q_ref), (order_in, order_ref))
        )
    ]
    for load in loads:
        load.start()

    barrier = pltpu.get_barrier_semaphore()
    peers = [at_head(r) for r in (1, 2, 3)]
    peers += [at_next(0), at_next(1), (before, z, head), (before, ring + z, head)]
    peers += [at_z(1), at_z(-1), y_peer]
    for peer in peers:
        pl.semaphore_signal(barrier, inc=1, device_id=peer, device_id_type=MESH)
    loads[0].wait()
    loads[1].wait()
    kv_in[:, 0] = jnp.swapaxes(k_ref[...], 0, 1)
    v_rows = jnp.swapaxes(v_ref[...], 0, 1)
    for x in range(heads):
        kv_in[x, 1] = v_rows[x].T
    pl.semaphore_wait(barrier, len(peers))

    def remote(src, dst, send, recv, peer):
        return pltpu.make_async_remote_copy(
            src_ref=src, dst_ref=dst, send_sem=send, recv_sem=recv,
            device_id=peer, device_id_type=MESH,
        )

    def kv_copy(r):
        there = (head + r) % heads
        return remote(kv_in.at[there], own.at[:, head], x_send.at[r], x_recv.at[r], at_head(r))

    def q_copy(r):
        there = (head + r) % heads
        return remote(q_in.at[there], qbuf.at[heads - r], q_send.at[r], q_recv.at[r], at_head(r))

    for r in (1, 3, 2):
        kv_copy(r).start()
    loads[2].wait()
    q_in[...] = jnp.swapaxes(q_ref[...], 0, 1).reshape(q_in.shape)
    for r in (1, 3, 2):
        q_copy(r).start()
    loads[3].wait()

    def first_copy(r, n):
        p = (head + r) % heads
        src, dst, y_there = (
            (own.at[1, p], vbuf.at[0, z, p], near),
            (own.at[0, p], kbuf.at[0, z, p], near),
            (own.at[0, p], kbuf.at[1, z, p], 1 - near),
        )[n]
        return remote(src, dst, first_send.at[n, r], first_recv.at[n, p], at_next(y_there))

    def send_first(r):
        if r:
            kv_copy(heads - r).wait_recv()
        for n in range(3):
            first_copy(r, n).start()

    def k_copy(way, kind, origin):
        peer = at_z(turn if way == 0 else -turn)
        return remote(
            kbuf.at[kind, origin], kbuf.at[kind, origin],
            k_send.at[way, kind, origin], k_recv.at[kind, origin], peer,
        )

    def v_copy(way, origin):
        peer = at_z(turn if way == 0 else -turn)
        return remote(
            vbuf.at[0, origin], vbuf.at[0, origin],
            v_send.at[way, origin], v_recv.at[0, origin], peer,
        )

    def y_copy(origin):
        return remote(
            vbuf.at[0, origin], vbuf.at[1, origin], y_send.at[origin], v_recv.at[1, origin], y_peer
        )

    def origin_of(way, step):
        by = turn * step
        return (z - by + ring) % ring if way == 0 else (z + by + ring) % ring

    def pass_first(r, ns):
        p = (head + r) % heads
        for n in ns:
            first_copy(r, n).wait_recv()
            for way in (0, 1):
                peer = at_z(turn if way == 0 else -turn)
                if n == 0:
                    buf, send, recv = vbuf.at[0, z, p], v_send.at[way, z], v_recv.at[0, z]
                else:
                    buf = kbuf.at[n - 1, z, p]
                    send, recv = k_send.at[way, n - 1, z], k_recv.at[n - 1, z]
                remote(buf, buf, send, recv, peer).start()

    def last_step(way, kind):
        return ring // 2 if way == kind else ring // 2 - 1

    def v_event(way, step):
        origin = origin_of(way, step)
        v_copy(way, origin).wait_recv()
        pl.when(step < last_step(way, 0))(lambda: v_copy(way, origin).start())
        y_copy(origin).start()

    def k_event(way, kind, step):
        origin = origin_of(way, step)
        k_copy(way, kind, origin).wait_recv()
        pl.when(step < last_step(way, kind))(lambda: k_copy(way, kind, origin).start())

    def k_events(kind, step):
        k_event(0, kind, step)
        k_event(1, kind, step)

    def y_event(origin):
        remote(
            vbuf.at[1, origin], vbuf.at[1, origin], y_send.at[origin], v_recv.at[1, origin], y_peer
        ).wait_recv()

    def slot_of(c):
        step, place = c // 4, c % 4
        kind = jnp.where(step == 0, place - 2, jnp.where(step == ring // 2, place, place // 2))
        sign = 1 - 2 * (place % 2)
        return kind, (z - turn * sign * step + ring) % ring

    def halves_of(c):
        kind, origin = slot_of(c)
        y_there = jnp.where((core + kind) % 2 == 1, y, 1 - y)
        block = before * inners + y_there * ring + origin
        return order_ref[2 * block], order_ref[2 * block + 1]

    here = 2 * (outer * inners + inner)
    here_order = (order_ref[here], order_ref[here + 1])

    def tile_order(r):
        return jnp.where((head + r) % heads < 2, here_order[0], here_order[1])

    scores = (s0, s1)
    columns = group * part

    def score(k_rows, r):
        q = qbuf[r]
        return lax.dot_general(k_rows, q, NT, preferred_element_type=jnp.float32) * scale

    def ahead(c, r, slot):
        kind, origin = slot_of(c)
        for h in range(2):
            k_rows = kbuf[kind, origin, 2 * h : 2 * h + 2].reshape(half, head_dim)
            s = score(k_rows, r)
            scores[slot][h * half : (h + 1) * half] = s
            tile_max[slot, h] = jnp.max(s, axis=0, keepdims=True)

    def ahead_own(r, slot):
        token = lax.broadcasted_iota(jnp.int32, (1, columns), 1) % part
        q_token = ((head + r) % 2) * part + token
        q_pos = tile_order(r) * half + q_token
        for h in range(2):
            k_rows = own[0, 2 * h : 2 * h + 2].reshape(half, head_dim)
            k_pos = here_order[h] * half + lax.broadcasted_iota(jnp.int32, (half, 1), 0)
            s = jnp.where(k_pos <= q_pos, score(k_rows, r), NEG)
            scores[slot][h * half : (h + 1) * half] = s
            tile_max[slot, h] = jnp.max(s, axis=0, keepdims=True)

    def absorb(v_parts, hidden, r, slot, first=False):
        new = jnp.maximum(tile_max[slot, 0] - hidden[0], tile_max[slot, 1] - hidden[1])
        if not first:
            old = m_ref[r]
            new = jnp.maximum(old, new)
            shrink = jnp.exp2(old - new)
        m_ref[r] = new
        weights = jnp.concatenate(
            [
                jnp.exp2(scores[slot][h * half : (h + 1) * half] - (new + hidden[h]))
                for h in range(2)
            ],
            axis=0,
        ).astype(jnp.bfloat16)
        v = jnp.concatenate(v_parts, axis=1)
        v = jnp.concatenate([v, jnp.ones((16, keys), jnp.bfloat16)], axis=0)
        add = lax.dot_general(v, weights, NN, preferred_element_type=jnp.float32)
        add = add[: head_dim + 8]
        acc_ref[r] = add if first else acc_ref[r] * shrink + add

    def now(c, r, slot):
        kind, origin = slot_of(c)
        mine = tile_order(r)
        hidden = [jnp.where(k < mine, 0.0, -NEG) for k in halves_of(c)]
        absorb([vbuf[kind, origin, x] for x in range(heads)], hidden, r, slot)

    def now_own(r, slot):
        absorb([own[1, x] for x in range(heads)], (0.0, 0.0), r, slot, first=True)

    cut = columns // 2

    def out_copy(r, n):
        rows = pl.ds(n * cut, cut)
        return remote(
            outbuf.at[r, rows], got.at[head, rows], o_send.at[r, n], o_recv.at[r, n], at_head(r)
        )

    def finish(r):
        total = acc_ref[r, head_dim : head_dim + 1]
        rows = [
            (acc_ref[r, :head_dim, at : at + cut] / total[:, at : at + cut]).astype(jnp.bfloat16).T
            for at in (0, cut)
        ]
        there = (head + r) % heads
        for n in range(2):
            if r == 0:
                got[head, n * cut : (n + 1) * cut] = rows[n]
            else:
                outbuf[r, n * cut : (n + 1) * cut] = rows[n]
                out_copy(r, n).start()
        logs = (m_ref[r] + jnp.log2(total)) * LN2
        for g in range(group):
            log_ref[g : g + 1, pl.ds(pl.multiple_of(there * part, part), part)] = logs[
                :, g * part : (g + 1) * part
            ]

    own[0, head] = kv_in[head, 0]
    own[1, head] = kv_in[head, 1]
    send_first(0)
    qbuf[0] = q_in[head]
    send_first(ARRIVAL[1])
    pass_first(ARRIVAL[0], (0, 1))
    send_first(ARRIVAL[2])
    pass_first(ARRIVAL[1], (0, 1))
    send_first(ARRIVAL[3])
    pass_first(ARRIVAL[2], (0, 1))
    pass_first(ARRIVAL[0], (2,))
    pass_first(ARRIVAL[1], (2,))
    pass_first(ARRIVAL[3], (0, 1))
    y_copy(z).start()
    pass_first(ARRIVAL[2], (2,))
    pass_first(ARRIVAL[3], (2,))

    def do_ahead(c, r, slot):
        if c == 0:
            if r:
                q_copy(heads - r).wait_recv()
            ahead_own(r, slot)
        else:
            ahead(c, r, slot)

    early = [(0, 0), (2, 0), (0, 1), (2, 1), (0, 3), (2, 3)]
    early += [(3, 0), (3, 1), (3, 3), (0, 2), (2, 2), (3, 2)]
    do_ahead(*early[0], 0)
    for n in range(11):
        if early[n + 1] == (0, 3):
            v_event(0, 1)
            v_event(1, 1)
        if early[n + 1] == (0, 2):
            k_events(0, 1)
        do_ahead(*early[n + 1], (n + 1) % 2)
        c, r = early[n]
        if (c, r) == (3, 0):
            y_event(z)
        if c == 0:
            now_own(r, n % 2)
        else:
            now(c, r, n % 2)

    def events(c):
        step, place = c // 4, c % 4

        @pl.when(jnp.logical_and(place == 0, step > 1))
        def _():
            k_events(0, step)

        @pl.when(place == K1_PLACE)
        def _():
            k_events(1, step)

        @pl.when(place == 2)
        def _():
            y_event(origin_of(0, step))

        @pl.when(place == 3)
        def _():
            y_event(origin_of(1, step))
            v_event(0, step + 1)
            pl.when(step < 3)(lambda: v_event(1, step + 1))

    def chunk(c, _):
        events(c)
        ahead(c, LOOP[0], 0)
        now(c - 1, LOOP[3], 1)
        for n in range(3):
            ahead(c, LOOP[n + 1], (n + 1) % 2)
            now(c, LOOP[n], n % 2)
        return 0

    lax.fori_loop(4, LAST, chunk, 0)

    if LAST < 15:
        y_event(origin_of(0, 3))
    if LAST < 16:
        y_event(origin_of(1, 3))
        v_event(0, 4)
    steps = [(c, r) for r in ORDER for c in range(LAST, 18)]
    last = len(steps) - 1
    for n in range(-1, last + 1):
        if n < last:
            if steps[n + 1] == (16, ORDER[0]):
                k_event(0, 0, ring // 2)
            if steps[n + 1] == (17, ORDER[0]):
                k_event(1, 1, ring // 2)
            ahead(*steps[n + 1], (n + 1) % 2)
        if n < 0:
            now(LAST - 1, LOOP[3], 1)
            continue
        c, r = steps[n]
        if (c, r) == (17, ORDER[0]):
            y_event(origin_of(0, ring // 2))
        now(c, r, n % 2)
        if c == 17:
            finish(r)

    for r in (1, 2, 3):
        out_copy(r, 0).wait_recv()
        out_copy(r, 1).wait_recv()
    out_ref[...] = jnp.swapaxes(got[...].reshape(heads * group, part, head_dim), 0, 1)
    for r in (1, 2, 3):
        out_copy(r, 0).wait_send()
        out_copy(r, 1).wait_send()
        kv_copy(r).wait_send()
        q_copy(r).wait_send()
    for r in range(heads):
        for n in range(3):
            first_copy(r, n).wait_send()
    y_copy(z).wait_send()
    for way in (0, 1):
        v_copy(way, z).wait_send()
        for kind in (0, 1):
            k_copy(way, kind, z).wait_send()

    def ended(step, _):
        for way in (0, 1):
            origin = origin_of(way, step)
            y_copy(origin).wait_send()
            pl.when(step < last_step(way, 0))(lambda: v_copy(way, origin).wait_send())
            for kind in (0, 1):
                pl.when(step < last_step(way, kind))(
                    lambda: k_copy(way, kind, origin).wait_send()
                )
        return 0

    lax.fori_loop(1, 4, ended, 0)
    y_copy(origin_of(0, ring // 2)).wait_send()


def body(queries, keys, values, block_order):
    heads = lax.axis_size("head")
    inners = lax.axis_size("inner")
    part, q_heads, head_dim = queries.shape
    group = q_heads // heads
    ring = inners // 2
    columns = group * part
    block = heads * part
    bf16, f32 = jnp.bfloat16, jnp.float32
    dma = pltpu.SemaphoreType.DMA
    vmem = pl.BlockSpec(memory_space=pltpu.VMEM)
    return pl.pallas_call(
        functools.partial(kernel, group, ring),
        out_shape=(
            jax.ShapeDtypeStruct(queries.shape, bf16),
            jax.ShapeDtypeStruct((group, block), f32),
        ),
        in_specs=[pl.BlockSpec(memory_space=pltpu.HBM)] * 4,
        out_specs=(vmem, vmem),
        scratch_shapes=[
            pltpu.SMEM(block_order.shape, jnp.int32),
            pltpu.VMEM(queries.shape, bf16),
            pltpu.VMEM(keys.shape, bf16),
            pltpu.VMEM(values.shape, bf16),
            pltpu.VMEM((heads, columns, head_dim), bf16),
            pltpu.VMEM((heads, 2, part, head_dim), bf16),
            pltpu.VMEM((heads, columns, head_dim), bf16),
            pltpu.VMEM((heads, columns, head_dim), bf16),
            pltpu.VMEM((2, heads, part, head_dim), bf16),
            pltpu.VMEM((2, ring, heads, part, head_dim), bf16),
            pltpu.VMEM((2, ring, heads, head_dim, part), bf16),
            pltpu.VMEM((heads, columns, head_dim), bf16),
            pltpu.VMEM((heads, 1, columns), f32),
            pltpu.VMEM((heads, head_dim + 8, columns), f32),
            pltpu.VMEM((block, columns), f32),
            pltpu.VMEM((block, columns), f32),
            pltpu.VMEM((2, 2, 1, columns), f32),
            dma((heads,)),
            dma((heads,)),
            dma((heads,)),
            dma((heads,)),
            dma((3, heads)),
            dma((3, heads)),
            dma((2, ring)),
            dma((2, ring)),
            dma((2, 2, ring)),
            dma((2, ring)),
            dma((ring,)),
            dma((heads, 2)),
            dma((heads, 2)),
            dma((4,)),
        ],
        compiler_params=pltpu.CompilerParams(
            collective_id=0, has_side_effects=True, vmem_limit_bytes=60 * 2**20
        ),
        cost_estimate=pl.CostEstimate(
            flops=4 * q_heads * block * (2 * ring + 1) * block * head_dim // heads,
            bytes_accessed=4 * 2**20,
            transcendentals=q_heads * block * (2 * ring + 1) * block // heads,
        ),
    )(block_order, queries, keys, values)


def solution(mesh):
    spread = P(("outer", "inner", "head"), None, None)
    return jax.shard_map(
        body,
        mesh=mesh,
        in_specs=(spread, spread, spread, P()),
        out_specs=(spread, P("head", ("outer", "inner"))),
        check_vma=False,
    )
```
